32 devices in a mesh: groups: 1, seq: 4 (over z), tensor: 4 (over y, x), section: 2 (over core).
Axes of the slice: x: 2, y: 2, z: 4, core: 2. Of those that a mesh axis runs over, the one named last changes fastest.
Arguments:
- prompts: bfloat16 [1024, 8192], P(('groups', 'seq', 'section')), may hold values from -6 to 6
- kv_weight: bfloat16 [8192, 2, 1024], P(('seq', 'section'), None, 'tensor'), may hold values from -0.0625 to 0.0625
- lengths: int32 [64], P('groups'), may hold values from 1 to 512, 1024 in all
- piece_owner: int32 [32], P('groups'), may hold values from 0 to 7, as said below
- piece_slot: int32 [32], P('groups'), may hold values from 0 to 7, as said below
- queries: bfloat16 [256, 8192], P('groups', 'tensor'), may hold values from -128 to 128
- decode_key_value: bfloat16 [256, 2, 1024], P('groups', None, 'tensor'), may hold values from -16 to 16
Outputs:
- cache: bfloat16 [2048, 2, 1024], P(('groups', 'seq', 'section'), None, 'tensor')
- attended: bfloat16 [256, 8192], P('groups', 'tensor')
The draws below stay inside these ranges and needn't reach their ends.
Inputs may be any that keep to these rules, and one draw needn't show every extreme that they name: `piece_owner`: the pieces of one device (4 aligned pieces in a row) go to distinct owners; an owner receives at most 8 pieces, and some owner receives exactly 8. `piece_slot`: the pieces of one owner hold distinct slots; an owner with n pieces uses slots 0 to n - 1.
All inputs are finite; a program needn't handle non-finite values.
Results may differ from the reference program's by a relative error of at most 0.0015.
The reference program's roundings to bfloat16 on the way count: a program that leaves them out, or rounds other values in their place, can miss the bound.
Values may be sent and summed in bfloat16 or wider, within the bound.
A program may use at most 64 MiB of HBM per device.

```python
import math
import jax
import jax.numpy as jnp
import numpy as np
from jax import lax

D = 8192
QUERY_HEADS = 64
KEY_VALUE_HEADS = 8
HEAD_SIZE = 128
DECODE_STEPS = 4
REQUEST_COUNT = 64
SHARDS = 8
TOKENS = 1024
PIECE = 32
PIECES = 32
OWNER_CACHE_ROWS = 256
CACHE = 2048
KVW = 1024
DECODE_ROWS = 256
LEN_MOST = 512


def assign_pieces(key):
    key = jax.random.fold_in(key, 23)
    output_parts = jax.random.split(key, 3)
    half = SHARDS // 2
    spread = jax.random.randint(output_parts[0], (half,), 0, half + 1)
    spread = spread.at[0].set(half)
    loads = jnp.stack([half + spread, half - spread], axis=1).reshape(SHARDS).astype(jnp.int32)
    labels = jax.random.permutation(output_parts[1], SHARDS).astype(jnp.int32)
    senders = jax.random.permutation(output_parts[2], SHARDS).astype(jnp.int32)
    ends = jnp.cumsum(loads).astype(jnp.int32)
    entry = jnp.arange(PIECES, dtype=jnp.int32)
    which = jnp.sum((entry[:, None] >= ends[None, :]).astype(jnp.int32), axis=1)
    rank = entry - (ends - loads)[which]
    placed = senders[entry % SHARDS] * half + entry // SHARDS
    owner = jnp.zeros((PIECES,), jnp.int32).at[placed].set(labels[which])
    slot = jnp.zeros((PIECES,), jnp.int32).at[placed].set(rank)
    return (owner, slot)


def decode_pair(key, strength):
    key = jax.random.fold_in(key, 11)
    output_parts = jax.random.split(key, 7)
    fresh_entries = jax.random.normal(output_parts[0], (DECODE_ROWS, 2, KVW), jnp.float32)
    asked_rows = jax.random.normal(output_parts[1], (DECODE_ROWS, QUERY_HEADS * HEAD_SIZE), jnp.float32)
    reshaped_rows = fresh_entries[:, 0].reshape(REQUEST_COUNT, DECODE_STEPS, KEY_VALUE_HEADS, HEAD_SIZE)
    second = reshaped_rows[:, 1]
    reshaped_rows = reshaped_rows.at[:, 1].set(second)
    chosen = (jax.random.randint(output_parts[3], (REQUEST_COUNT,), 0, 4) == 0).astype(jnp.float32)
    asked_rows = asked_rows.reshape(REQUEST_COUNT, DECODE_STEPS, QUERY_HEADS, HEAD_SIZE)
    loud = (jax.random.randint(output_parts[5], (REQUEST_COUNT,), 0, 4) == 1).astype(jnp.float32)
    boost = 10.0 + 35.0 * jax.random.uniform(output_parts[6], (REQUEST_COUNT,), jnp.float32)
    multiplier = 1.0 + strength * (1.0 - chosen) * loud * (boost - 1.0)
    asked_rows = asked_rows * multiplier[:, None, None, None]
    fresh_entries = fresh_entries.at[:, 0].set(reshaped_rows.reshape(DECODE_ROWS, KVW))
    return (jnp.clip(asked_rows.reshape(DECODE_ROWS, QUERY_HEADS * HEAD_SIZE), -128.0, 128.0), jnp.clip(fresh_entries, -16.0, 16.0))


def draw_piece_owner(key, part):
    return assign_pieces(key)[0]


def draw_piece_slot(key, part):
    return assign_pieces(key)[1]


def draw_queries(key, part):
    return decode_pair(key, 0.0)[0].astype(jnp.bfloat16)


def draw_decode_key_value(key, part):
    return decode_pair(key, 0.0)[1].astype(jnp.bfloat16)


def block_scale(stream_key, shape, cuts, low, top_value):
    def one(position, parts):
        steps = jax.random.uniform(jax.random.fold_in(jax.random.fold_in(stream_key, 6), position), (parts,), jnp.float32, low / len(cuts), top_value / len(cuts))
        return jnp.repeat(jnp.exp(steps), shape[position] // parts).reshape((-1,) + (1,) * (len(shape) - position - 1))

    level = one(*cuts[0])
    for cut in cuts[1:]:
        level = level * one(*cut)
    return level


def split_up(number_of, total, most, lean):
    weights = [(1 << 20) // math.isqrt(rank ** lean) + 1 for rank in range(2, number_of + 1)]
    spare, holding = total - most - (number_of - 1), [1] * (number_of - 1)
    while spare > 0:
        movable = [i for i in range(number_of - 1) if holding[i] < most]
        whole, left = sum([weights[i] for i in movable]), spare
        for i in movable:
            more = min(most - holding[i], max(1, left * weights[i] // whole), spare)
            holding[i] = holding[i] + more
            spare = spare - more
    return np.array([most] + holding)


def uneven(stream_key, amount, total, most, slope):
    if amount == 2:
        one = jax.random.randint(stream_key, (), max(1, total - most), min(most, total - 1) + 1)
        return jnp.stack([one, total - one])
    sizes = jnp.asarray(split_up(amount, total, most, slope), jnp.int32)
    twos = (amount - 1) // 2
    donor, sink = sizes[1:1 + 2 * twos:2], sizes[2:2 + 2 * twos:2]
    margin = jnp.minimum(donor - 1, most - sink)
    shifted = jax.random.randint(jax.random.fold_in(stream_key, 1), (twos,), 0, 1 << 20) % (margin + 1)
    sizes = sizes.at[1:1 + 2 * twos:2].set(donor - shifted).at[2:2 + 2 * twos:2].set(sink + shifted)
    return sizes[jax.random.permutation(jax.random.fold_in(stream_key, 2), amount)]


def centred(rng, dims, scale, bound, cuts=(), held_as=jnp.bfloat16):
    factor_of = block_scale(rng, dims, cuts, -0.22, 0.18) if cuts else 1.0
    array = jax.random.normal(rng, dims, jnp.float32) * scale * factor_of
    return jnp.minimum(jnp.maximum(array, -bound), bound).astype(held_as)


def setup_inputs(seed: int = 0, part: int = 0) -> dict:
    key_of = jax.random.split(jax.random.key(seed), 8)
    part_keys = jax.random.split(jax.random.fold_in(key_of[7], part), 8)
    prompts = centred(part_keys[0], (TOKENS, D), 1.0, 6.0, ((0, 8),))
    kv_weight = centred(key_of[1], (D, 2, KVW), D ** -0.5, 0.0625, ((0, 8), (2, 4)))
    lengths = uneven(part_keys[2], REQUEST_COUNT, TOKENS, LEN_MOST, 2).astype(jnp.int32)
    piece_owner = draw_piece_owner(jax.random.fold_in(jax.random.fold_in(key_of[7], part), 71), part)
    piece_slot = draw_piece_slot(jax.random.fold_in(jax.random.fold_in(key_of[7], part), 71), part)
    queries = draw_queries(jax.random.fold_in(jax.random.fold_in(key_of[7], part), 71), part)
    decode_key_value = draw_decode_key_value(jax.random.fold_in(jax.random.fold_in(key_of[7], part), 71), part)
    return {"prompts": prompts, "kv_weight": kv_weight, "lengths": lengths, "piece_owner": piece_owner, "piece_slot": piece_slot, "queries": queries, "decode_key_value": decode_key_value}


masked_value = -1e30


def partial_softmax(scores, allowed):
    highest = jnp.max(jnp.where(allowed, scores, masked_value), axis=-1)
    weights = jnp.where(allowed, jnp.exp(scores - highest[..., None]), 0.0)
    total = jnp.sum(weights, axis=-1)
    rounded = lax.optimization_barrier(weights.astype(jnp.bfloat16)).astype(jnp.float32)
    return highest, total, rounded


def join_parts(first, second):
    top = jnp.maximum(first[0], second[0])
    left = jnp.exp(first[0] - top)
    right = jnp.exp(second[0] - top)
    return (top, first[1] * left + second[1] * right, first[2] * left[..., None] + second[2] * right[..., None])


def reference(prompts, kv_weight, lengths, piece_owner, piece_slot, queries, decode_key_value):
    fresh_entries = jnp.dot(prompts, kv_weight.reshape(D, 2 * KVW), preferred_element_type=jnp.float32)
    fresh_entries = fresh_entries.astype(jnp.bfloat16).reshape(TOKENS, 2, KVW)
    token = jnp.arange(TOKENS, dtype=jnp.int32)
    piece_index = token // PIECE
    target = piece_owner[piece_index] * OWNER_CACHE_ROWS + piece_slot[piece_index] * PIECE + token % PIECE
    cache = jnp.zeros((CACHE, 2, KVW), jnp.bfloat16).at[target].set(fresh_entries)
    ends = jnp.cumsum(lengths).astype(jnp.int32)
    request = jnp.sum((token[:, None] >= ends[None, :]).astype(jnp.int32), axis=1).astype(jnp.int32)
    slot_request = jnp.full((CACHE,), -1, jnp.int32).at[target].set(request)
    query_group = QUERY_HEADS // KEY_VALUE_HEADS
    scale = HEAD_SIZE ** -0.5
    asked_rows = queries.astype(jnp.float32).reshape(DECODE_ROWS, KEY_VALUE_HEADS, query_group, HEAD_SIZE)
    row_request = jnp.arange(DECODE_ROWS, dtype=jnp.int32) // DECODE_STEPS
    asked_fresh_rows = asked_rows.reshape(REQUEST_COUNT, DECODE_STEPS, KEY_VALUE_HEADS, query_group, HEAD_SIZE)
    fresh_key_rows = decode_key_value[:, 0].astype(jnp.float32).reshape(REQUEST_COUNT, DECODE_STEPS, KEY_VALUE_HEADS, HEAD_SIZE)
    fresh_value_rows = decode_key_value[:, 1].astype(jnp.float32).reshape(REQUEST_COUNT, DECODE_STEPS, KEY_VALUE_HEADS, HEAD_SIZE)
    new_scores = jnp.einsum("rtgjd,rsgd->rtgjs", asked_fresh_rows, fresh_key_rows) * scale
    steps_range = jnp.arange(DECODE_STEPS, dtype=jnp.int32)
    causal = (steps_range[:, None] >= steps_range[None, :])[None, :, None, None, :]
    fresh_maximum, fresh_total_sum, new_weights = partial_softmax(new_scores, causal)
    fresh_weight_sum = jnp.einsum("rtgjs,rsgd->rtgjd", new_weights, fresh_value_rows)
    start_index = (fresh_maximum.reshape(DECODE_ROWS, KEY_VALUE_HEADS, query_group), fresh_total_sum.reshape(DECODE_ROWS, KEY_VALUE_HEADS, query_group), fresh_weight_sum.reshape(DECODE_ROWS, KEY_VALUE_HEADS, query_group, HEAD_SIZE))

    def owner_step(carry, owner):
        cache_block = lax.dynamic_slice_in_dim(cache, (owner * OWNER_CACHE_ROWS).astype(jnp.int32), OWNER_CACHE_ROWS, 0).astype(jnp.float32)
        holder_key_rows = cache_block[:, 0].reshape(OWNER_CACHE_ROWS, KEY_VALUE_HEADS, HEAD_SIZE)
        holder_value_rows = cache_block[:, 1].reshape(OWNER_CACHE_ROWS, KEY_VALUE_HEADS, HEAD_SIZE)
        owner_request = lax.dynamic_slice_in_dim(slot_request, (owner * OWNER_CACHE_ROWS).astype(jnp.int32), OWNER_CACHE_ROWS, 0)
        scores = jnp.einsum("rgjd,cgd->rgjc", asked_rows, holder_key_rows) * scale
        allowed = (owner_request[None, :] == row_request[:, None])[:, None, None, :]
        highest, total, weights = partial_softmax(scores, allowed)
        summed = jnp.einsum("rgjc,cgd->rgjd", weights, holder_value_rows)
        return join_parts(carry, (highest, total, summed)), None

    final, unused = lax.scan(owner_step, start_index, jnp.arange(SHARDS, dtype=jnp.int32))
    attended = (final[2] / final[1][..., None]).astype(jnp.bfloat16).reshape(DECODE_ROWS, QUERY_HEADS * HEAD_SIZE)
    return cache, attended
```

```python
import functools

import jax
import jax.numpy as jnp
from jax import lax
from jax.experimental import pallas as pl
from jax.experimental.pallas import tpu as pltpu
from jax.sharding import PartitionSpec as P

HEAD_SIZE = 128
DECODE_STEPS = 4


masked_value = -1e30


def partial_softmax(scores, allowed):
    highest = jnp.max(jnp.where(allowed, scores, masked_value), axis=-1)
    weights = jnp.where(allowed, jnp.exp(scores - highest[..., None]), 0.0)
    return (highest, jnp.sum(weights, axis=-1), weights.astype(jnp.bfloat16))


def join_parts(first, second):
    top = jnp.maximum(first[0], second[0])
    left = jnp.exp(first[0] - top)
    right = jnp.exp(second[0] - top)
    return (
        top,
        first[1] * left + second[1] * right,
        first[2] * left[..., None] + second[2] * right[..., None],
    )


def per_device(prompts, kv_weight, lengths, piece_owner, piece_slot, queries, decode_key_value):
    shards = lax.axis_size(("seq", "section"))
    sender = lax.axis_index(("seq", "section"))
    tok_rows = prompts.shape[0]
    local_kv = kv_weight.shape[2]
    per_sender = shards // 2
    piece_len = tok_rows // per_sender
    cache_block = lax.all_gather(kv_weight, ("seq", "section"), axis=0, tiled=True)
    flat = cache_block.reshape(cache_block.shape[0], 2 * local_kv)
    summed = jnp.dot(prompts, flat, preferred_element_type=jnp.float32)
    fresh_entries = summed.astype(jnp.bfloat16).reshape(tok_rows, 2, local_kv)
    pieces = fresh_entries.reshape(per_sender, piece_len * 2 * local_kv)
    my_owners = lax.dynamic_slice_in_dim(piece_owner, sender * per_sender, per_sender)
    owner_range = jnp.arange(shards, dtype=jnp.int32)
    targets = (owner_range[:, None] == my_owners[None, :]).astype(jnp.bfloat16)
    outgoing = jnp.dot(targets, pieces, preferred_element_type=jnp.float32).astype(jnp.bfloat16)
    arrived = lax.all_to_all(outgoing, ("seq", "section"), split_axis=0, concat_axis=0, tiled=True)
    piece_ids = jnp.arange(piece_owner.shape[0], dtype=jnp.int32)
    matched = (
        (piece_owner == sender)[None, :] & (piece_slot[None, :] == owner_range[:, None])
    ).astype(jnp.int32)
    from_sender = jnp.sum(matched.reshape(shards, shards, per_sender), axis=2).astype(jnp.bfloat16)
    cache_local = jnp.dot(from_sender, arrived, preferred_element_type=jnp.float32).astype(
        jnp.bfloat16
    )
    cache_local = cache_local.reshape(shards * piece_len, 2, local_kv)
    has_piece = jnp.sum(matched, axis=1)
    first_token = jnp.sum(matched * piece_ids[None, :], axis=1) * piece_len
    slot_token = (first_token[:, None] + jnp.arange(piece_len, dtype=jnp.int32)[None, :]).reshape(
        -1
    )
    ends = jnp.cumsum(lengths)
    token_request = jnp.sum((slot_token[:, None] >= ends[None, :]).astype(jnp.int32), axis=1)
    filled = jnp.repeat(has_piece > 0, piece_len)
    slot_request = jnp.where(filled, token_request, -1)
    rows = queries.shape[0]
    kv_heads = local_kv // HEAD_SIZE
    query_group = queries.shape[1] // (kv_heads * HEAD_SIZE)
    scale = HEAD_SIZE ** (-0.5)
    asked_rows = queries.reshape(rows, kv_heads, query_group, HEAD_SIZE)
    cache_keys = cache_local[:, 0].reshape(-1, kv_heads, HEAD_SIZE)
    cache_values = cache_local[:, 1].reshape(-1, kv_heads, HEAD_SIZE)
    scores = (
        jnp.einsum("rgjd,cgd->rgjc", asked_rows, cache_keys, preferred_element_type=jnp.float32)
        * scale
    )
    row_request = jnp.arange(rows, dtype=jnp.int32) // DECODE_STEPS
    allowed = (slot_request[None, :] == row_request[:, None])[:, None, None, :]
    highest, total, weights = partial_softmax(scores, allowed)
    weighted = jnp.einsum(
        "rgjc,cgd->rgjd", weights, cache_values, preferred_element_type=jnp.float32
    )
    requests = rows // DECODE_STEPS
    asked_fresh_rows = queries.reshape(requests, DECODE_STEPS, kv_heads, query_group, HEAD_SIZE)
    fresh_key_rows = decode_key_value[:, 0].reshape(requests, DECODE_STEPS, kv_heads, HEAD_SIZE)
    fresh_value_rows = decode_key_value[:, 1].reshape(requests, DECODE_STEPS, kv_heads, HEAD_SIZE)
    new_scores = (
        jnp.einsum(
            "rtgjd,rsgd->rtgjs",
            asked_fresh_rows,
            fresh_key_rows,
            preferred_element_type=jnp.float32,
        )
        * scale
    )
    steps_range = jnp.arange(DECODE_STEPS, dtype=jnp.int32)
    causal = (steps_range[:, None] >= steps_range[None, :])[None, :, None, None, :]
    fresh_maximum, fresh_total_sum, new_weights = partial_softmax(new_scores, causal)
    fresh_weight_sum = jnp.einsum(
        "rtgjs,rsgd->rtgjd", new_weights, fresh_value_rows, preferred_element_type=jnp.float32
    )
    new_part = (
        fresh_maximum.reshape(rows, kv_heads, query_group),
        fresh_total_sum.reshape(rows, kv_heads, query_group),
        fresh_weight_sum.reshape(rows, kv_heads, query_group, HEAD_SIZE),
    )
    top = lax.pmax(highest, ("seq", "section"))
    group_factor = jnp.exp(highest - top)
    total_sum, weighted_sum = lax.psum(
        (total * group_factor, weighted * group_factor[..., None]), ("seq", "section")
    )
    owners_part = (top, total_sum, weighted_sum)
    final = join_parts(owners_part, new_part)
    attended = (
        (final[2] / final[1][..., None])
        .astype(jnp.bfloat16)
        .reshape(rows, kv_heads * query_group * HEAD_SIZE)
    )
    return (cache_local, attended)


MESH = pl.DeviceIdType.MESH


def project_kernel(
    chips,
    planes,
    prompts,
    weight,
    fresh,
    gathered,
    mine,
    theirs,
    from_sibling,
    summed,
    reduced,
    own_sem,
    send_sem,
    plane_send_sem,
    sum_send_sem,
    fresh_send_sem,
    line_sem,
    plane_sem,
    sibling_sem,
    reduce_sem,
    fresh_sem,
    fresh_sibling_sem,
):
    z = lax.axis_index("seq")
    t = lax.axis_index("tensor")
    c = lax.axis_index("section")
    other = 1 - c
    me = z * 2 + c
    piece = prompts.shape[1]
    depth = weight.shape[0]
    half = weight.shape[1] // 2
    rows = 2 * planes * piece

    def at(seq, tensor, section):
        return {"seq": seq, "tensor": tensor, "section": section}

    def remote(src, dst, ssem, rsem, where):
        return pltpu.make_async_remote_copy(
            src_ref=src,
            dst_ref=dst,
            send_sem=ssem,
            recv_sem=rsem,
            device_id=where,
            device_id_type=MESH,
        )

    barrier = pltpu.get_barrier_semaphore()
    for d in range(1, chips):
        for s in range(2):
            pl.semaphore_signal(
                barrier, inc=1, device_id=at(lax.rem(z + d, chips), t, s), device_id_type=MESH
            )
    for d in range(1, planes):
        pl.semaphore_signal(
            barrier, inc=1, device_id=at(z, lax.rem(t + d, planes), c), device_id_type=MESH
        )
    pl.semaphore_signal(barrier, inc=1, device_id=at(z, t, other), device_id_type=MESH)

    def columns(k):
        return pl.ds(pl.multiple_of(k * depth, depth), depth)

    own = pltpu.make_async_copy(
        prompts.at[:, :, columns(me)], gathered.at[pl.ds(me * planes, planes)], own_sem
    )
    own.start()
    pl.semaphore_wait(barrier, 2 * (chips - 1) + planes)

    sends = []
    copy = remote(
        prompts.at[:, :, columns(z * 2 + other)],
        gathered.at[pl.ds(me * planes, planes)],
        send_sem.at[0],
        line_sem.at[me],
        at(z, t, other),
    )
    copy.start()
    sends.append(copy)
    for d in range(1, chips):
        zt = lax.rem(z + d, chips)
        for s in range(2):
            copy = remote(
                prompts.at[t, :, columns(zt * 2 + s)],
                gathered.at[me * planes + t],
                send_sem.at[2 * d - 1 + s],
                line_sem.at[me],
                at(zt, t, s),
            )
            copy.start()
            sends.append(copy)

    def forward(d):
        zs = lax.rem(z + chips - d, chips)
        for s in range(2):
            src = zs * 2 + s
            slot = src * planes + t
            remote(
                gathered.at[slot],
                gathered.at[slot],
                send_sem.at[0],
                line_sem.at[src],
                at(z, t, other),
            ).wait_recv()
            for e in range(1, planes):
                copy = remote(
                    gathered.at[slot],
                    gathered.at[slot],
                    plane_send_sem.at[d - 1, s, e - 1],
                    plane_sem.at[src, t],
                    at(z, lax.rem(t + e, planes), c),
                )
                copy.start()
                sends.append(copy)

    def multiply(d):
        zs = lax.rem(z + chips - d, chips)
        if d == 0:
            own.wait()
            sibling = pl.ds((z * 2 + other) * planes, planes)
            remote(
                gathered.at[sibling],
                gathered.at[sibling],
                send_sem.at[0],
                line_sem.at[z * 2 + other],
                at(z, t, other),
            ).wait_recv()
        else:
            for s in range(2):
                src = zs * 2 + s
                for e in range(1, planes):
                    te = lax.rem(t + e, planes)
                    slot = src * planes + te
                    remote(
                        gathered.at[slot],
                        gathered.at[slot],
                        send_sem.at[0],
                        plane_sem.at[src, te],
                        at(z, te, c),
                    ).wait_recv()
        left = gathered[pl.ds(zs * 2 * planes, 2 * planes)].reshape(rows, depth)
        theirs[d] = jnp.dot(
            left,
            weight[:, pl.ds(pl.multiple_of(other * half, half), half)],
            preferred_element_type=jnp.float32,
        )
        copy = remote(
            theirs.at[d],
            from_sibling.at[d],
            sum_send_sem.at[0, d],
            sibling_sem.at[d],
            at(z, t, other),
        )
        copy.start()
        sends.append(copy)
        mine[d] = jnp.dot(
            left,
            weight[:, pl.ds(pl.multiple_of(c * half, half), half)],
            preferred_element_type=jnp.float32,
        )
        return copy

    def pass_on(d, copy):
        zs = lax.rem(z + chips - d, chips)
        copy.wait_recv()
        if d == 0:
            return
        summed[d - 1] = mine[d] + from_sibling[d]
        out = remote(
            summed.at[d - 1],
            reduced.at[d - 1],
            sum_send_sem.at[1, d],
            reduce_sem.at[d - 1],
            at(zs, t, c),
        )
        out.start()
        sends.append(out)
        return out

    outs = []
    held = multiply(0)
    for d in range(1, chips):
        forward(d)
        if d == 1:
            pass_on(0, held)
        else:
            later = multiply(d - 1)
            outs.append(pass_on(d - 1, later))
    held = multiply(chips - 1)
    outs.append(pass_on(chips - 1, held))

    total = mine[0] + from_sibling[0]
    for d in range(1, chips):
        outs[d - 1].wait_recv()
        total = total + reduced[d - 1]
    block = pl.ds(pl.multiple_of(z * rows, rows), rows)
    fresh[c, block] = total.astype(jnp.bfloat16)
    for d in range(1, chips):
        copy = remote(
            fresh.at[c, block],
            fresh.at[c, block],
            fresh_send_sem.at[0, d],
            fresh_sem.at[z],
            at(lax.rem(z + d, chips), t, c),
        )
        copy.start()
        sends.append(copy)
    for d in range(chips):
        zs = lax.rem(z + chips - d, chips)
        arrived = pl.ds(pl.multiple_of(zs * rows, rows), rows)
        if d > 0:
            remote(
                fresh.at[c, arrived],
                fresh.at[c, arrived],
                send_sem.at[0],
                fresh_sem.at[zs],
                at(z, t, other),
            ).wait_recv()
        copy = remote(
            fresh.at[c, arrived],
            fresh.at[c, arrived],
            fresh_send_sem.at[1, d],
            fresh_sibling_sem.at[zs],
            at(z, t, other),
        )
        copy.start()
        sends.append(copy)
    for d in range(chips):
        zs = lax.rem(z + chips - d, chips)
        arrived = pl.ds(pl.multiple_of(zs * rows, rows), rows)
        remote(
            fresh.at[other, arrived],
            fresh.at[other, arrived],
            send_sem.at[0],
            fresh_sibling_sem.at[zs],
            at(z, t, other),
        ).wait_recv()
    for copy in sends:
        copy.wait_send()


def project(prompts, weight, chips, planes):
    tok_rows, width = prompts.shape
    depth = weight.shape[0]
    half = weight.shape[1] // 2
    piece = tok_rows // planes
    rows = 2 * tok_rows
    shards = 2 * chips
    f32 = jnp.float32
    dma = pltpu.SemaphoreType.DMA
    return pl.pallas_call(
        functools.partial(project_kernel, chips, planes),
        out_shape=jax.ShapeDtypeStruct((2, chips * rows, half), jnp.bfloat16),
        in_specs=[
            pl.BlockSpec(memory_space=pl.ANY),
            pl.BlockSpec(memory_space=pltpu.VMEM),
        ],
        out_specs=pl.BlockSpec(memory_space=pltpu.VMEM),
        scratch_shapes=[
            pltpu.VMEM((shards * planes, piece, depth), jnp.bfloat16),
            pltpu.VMEM((chips, rows, half), f32),
            pltpu.VMEM((chips, rows, half), f32),
            pltpu.VMEM((chips, rows, half), f32),
            pltpu.VMEM((chips - 1, rows, half), f32),
            pltpu.VMEM((chips - 1, rows, half), f32),
            dma,
            dma((2 * chips - 1,)),
            dma((chips - 1, 2, planes - 1)),
            dma((2, chips)),
            dma((2, chips)),
            dma((shards,)),
            dma((shards, planes)),
            dma((chips,)),
            dma((chips - 1,)),
            dma((chips,)),
            dma((chips,)),
        ],
        compiler_params=pltpu.CompilerParams(
            collective_id=0, has_side_effects=True, vmem_limit_bytes=40 * 2**20
        ),
        name="project",
    )(prompts.reshape(planes, piece, width), weight)


TILE_REQUESTS = 8
TOKEN_BLOCK = 128


def attend_kernel(
    piece,
    lengths,
    piece_owner,
    piece_slot,
    fresh,
    queries,
    decode,
    cache,
    attended,
    ends,
    source,
    score,
    owner_max,
    weighted,
):
    owners = owner_max.shape[1]
    requests = lengths.shape[0]
    pieces = piece_owner.shape[0]
    tile_rows = TILE_REQUESTS * DECODE_STEPS
    kv_heads = fresh.shape[2] // HEAD_SIZE
    local = fresh.shape[2]
    group = queries.shape[1] // (kv_heads * HEAD_SIZE)
    lanes = group * tile_rows
    per_block = TOKEN_BLOCK // piece
    scale = HEAD_SIZE ** (-0.5)
    me = lax.axis_index("seq") * lax.axis_size("section") + lax.axis_index("section")

    ends[0] = 0

    def add_length(r, total):
        total = total + lengths[r]
        ends[r + 1] = total
        return total

    lax.fori_loop(0, requests, add_length, jnp.int32(0))

    slots = source.shape[0]
    for j in range(slots):
        source[j] = -1

    def place(p, carry):
        @pl.when(piece_owner[p] == me)
        def _():
            source[piece_slot[p]] = p

        return carry

    lax.fori_loop(0, pieces, place, 0)
    for j in range(slots):
        p = source[j]
        into = pl.ds(j * piece, piece)

        @pl.when(p >= 0)
        def _():
            rows = pl.ds(pl.multiple_of(p * piece, piece), piece)
            cache[into, :local] = fresh[0, rows]
            cache[into, local:] = fresh[1, rows]

        @pl.when(p < 0)
        def _():
            cache[into] = jnp.zeros((piece, 2 * local), cache.dtype)

    f32, bf16 = jnp.float32, jnp.bfloat16
    lane_row = lax.broadcasted_iota(jnp.int32, (1, lanes), 1) % tile_rows
    lane_request = lane_row // DECODE_STEPS
    token = lax.broadcasted_iota(jnp.int32, (TOKEN_BLOCK, lanes), 0)
    new_row = lax.broadcasted_iota(jnp.int32, (tile_rows, lanes), 0)
    new_mask = (new_row // DECODE_STEPS == lane_request) & (new_row <= lane_row)

    def outer(a, b):
        return lax.dot_general(a, b, (((1,), (1,)), ((), ())), preferred_element_type=f32)

    def inner(a, b):
        return lax.dot_general(a, b, (((0,), (0,)), ((), ())), preferred_element_type=f32)

    def tile(i, carry):
        first = i * TILE_REQUESTS
        begin = jnp.zeros((1, lanes), jnp.int32)
        end = jnp.zeros((1, lanes), jnp.int32)
        for r in range(TILE_REQUESTS):
            begin = jnp.where(lane_request == r, ends[first + r], begin)
            end = jnp.where(lane_request == r, ends[first + r + 1], end)
        low = ends[first] // TOKEN_BLOCK
        high = (ends[first + TILE_REQUESTS] + TOKEN_BLOCK - 1) // TOKEN_BLOCK
        rows = pl.ds(pl.multiple_of(i * tile_rows, tile_rows), tile_rows)
        asked = []
        for g in range(kv_heads):
            asked.append(
                jnp.concatenate(
                    [
                        queries[rows, (g * group + j) * HEAD_SIZE : (g * group + j + 1) * HEAD_SIZE]
                        for j in range(group)
                    ],
                    axis=0,
                )
            )
        owner_max[...] = jnp.full(owner_max.shape, masked_value, f32)

        def mask_of(b):
            place = token + b * TOKEN_BLOCK
            return (place >= begin) & (place < end)

        def scores(b, carry):
            allowed = mask_of(b)
            span = pl.ds(pl.multiple_of(b * TOKEN_BLOCK, TOKEN_BLOCK), TOKEN_BLOCK)
            for g in range(kv_heads):
                head = slice(g * HEAD_SIZE, (g + 1) * HEAD_SIZE)
                s = jnp.where(allowed, outer(fresh[0, span, head], asked[g]) * scale, masked_value)
                score[g, span] = s
                tops = jnp.max(s.reshape(per_block, piece, lanes), axis=1)
                for q in range(per_block):
                    o = pl.ds(piece_owner[b * per_block + q], 1)
                    owner_max[g, o] = jnp.maximum(owner_max[g, o], tops[q : q + 1])
            return carry

        lax.fori_loop(low, high, scores, 0)

        tops = []
        starts = []
        for g in range(kv_heads):
            keys = decode[rows, g * HEAD_SIZE : (g + 1) * HEAD_SIZE]
            values = decode[rows, local + g * HEAD_SIZE : local + (g + 1) * HEAD_SIZE]
            s = jnp.where(new_mask, outer(keys, asked[g]) * scale, masked_value)
            new_top = jnp.max(s, axis=0, keepdims=True)
            p = jnp.where(new_mask, jnp.exp(s - new_top), 0.0)
            top = jnp.maximum(new_top, jnp.max(owner_max[g], axis=0, keepdims=True))
            factor = jnp.exp(new_top - top)
            weighted[g] = inner(values, p.astype(bf16)) * factor
            tops.append(top)
            starts.append(jnp.sum(p, axis=0, keepdims=True) * factor)

        def weigh(b, totals):
            allowed = mask_of(b)
            span = pl.ds(pl.multiple_of(b * TOKEN_BLOCK, TOKEN_BLOCK), TOKEN_BLOCK)
            results = []
            for g in range(kv_heads):
                head = slice(g * HEAD_SIZE, (g + 1) * HEAD_SIZE)
                highest = jnp.concatenate(
                    [
                        jnp.broadcast_to(
                            owner_max[g, pl.ds(piece_owner[b * per_block + q], 1)], (piece, lanes)
                        )
                        for q in range(per_block)
                    ],
                    axis=0,
                )
                factor = jnp.exp(highest - tops[g])
                p = jnp.where(allowed, jnp.exp(score[g, span] - highest), 0.0)
                w = p.astype(bf16).astype(f32) * factor
                upper = w.astype(bf16)
                lower = (w - upper.astype(f32)).astype(bf16)
                values = fresh[1, span, head]
                weighted[g] += inner(values, upper) + inner(values, lower)
                results.append(totals[g] + jnp.sum(p * factor, axis=0, keepdims=True))
            return tuple(results)

        totals = lax.fori_loop(low, high, weigh, tuple(starts))
        for g in range(kv_heads):
            result = (weighted[g] / totals[g]).T.astype(bf16)
            for j in range(group):
                attended[rows, (g * group + j) * HEAD_SIZE : (g * group + j + 1) * HEAD_SIZE] = result[
                    j * tile_rows : (j + 1) * tile_rows
                ]
        return carry

    lax.fori_loop(0, requests // TILE_REQUESTS, tile, 0)


def attend(lengths, piece_owner, piece_slot, fresh, queries, decode, shards):
    tokens = fresh.shape[1]
    local = fresh.shape[2]
    piece = tokens // piece_owner.shape[0]
    slots = shards
    kv_heads = local // HEAD_SIZE
    group = queries.shape[1] // local
    lanes = group * TILE_REQUESTS * DECODE_STEPS
    smem = pl.BlockSpec(memory_space=pltpu.SMEM)
    vmem = pl.BlockSpec(memory_space=pltpu.VMEM)
    return pl.pallas_call(
        functools.partial(attend_kernel, piece),
        out_shape=(
            jax.ShapeDtypeStruct((slots * piece, 2 * local), jnp.bfloat16),
            jax.ShapeDtypeStruct(queries.shape, jnp.bfloat16),
        ),
        in_specs=[smem, smem, smem, vmem, vmem, vmem],
        out_specs=(vmem, vmem),
        scratch_shapes=[
            pltpu.SMEM((lengths.shape[0] + 1,), jnp.int32),
            pltpu.SMEM((slots,), jnp.int32),
            pltpu.VMEM((kv_heads, tokens, lanes), jnp.float32),
            pltpu.VMEM((kv_heads, shards, lanes), jnp.float32),
            pltpu.VMEM((kv_heads, HEAD_SIZE, lanes), jnp.float32),
        ],
        compiler_params=pltpu.CompilerParams(vmem_limit_bytes=32 * 2**20),
        name="attend",
    )(lengths, piece_owner, piece_slot, fresh, queries, decode)


def per_device_fused(
    mesh, prompts, kv_weight, lengths, piece_owner, piece_slot, queries, decode_key_value
):
    chips, planes = mesh.shape["seq"], mesh.shape["tensor"]
    depth, _, local = kv_weight.shape
    fresh = project(prompts, kv_weight.reshape(depth, 2 * local), chips, planes)
    cache, attended = attend(
        lengths,
        piece_owner,
        piece_slot,
        fresh,
        queries,
        decode_key_value.reshape(-1, 2 * local),
        2 * chips,
    )
    return cache.reshape(-1, 2, local), attended


def fits(mesh):
    return mesh.shape["section"] == 2 and mesh.shape["seq"] <= 4


def solution(mesh):
    placed = (
        P(("groups", "seq", "section"), None),
        P(("seq", "section"), None, "tensor"),
        P("groups"),
        P("groups"),
        P("groups"),
        P("groups", "tensor"),
        P("groups", None, "tensor"),
    )
    return jax.shard_map(
        functools.partial(per_device_fused, mesh) if fits(mesh) else per_device,
        mesh=mesh,
        in_specs=placed,
        out_specs=(P(("groups", "seq", "section"), None, "tensor"), P("groups", "tensor")),
        check_vma=False,
    )
```

```python
import functools

import jax
import jax.numpy as jnp
from jax import lax
from jax.experimental import pallas as pl
from jax.experimental.pallas import tpu as pltpu
from jax.sharding import PartitionSpec as P

HEAD_SIZE = 128
DECODE_STEPS = 4


masked_value = -1e30


def partial_softmax(scores, allowed):
    highest = jnp.max(jnp.where(allowed, scores, masked_value), axis=-1)
    weights = jnp.where(allowed, jnp.exp(scores - highest[..., None]), 0.0)
    return (highest, jnp.sum(weights, axis=-1), weights.astype(jnp.bfloat16))


def join_parts(first, second):
    top = jnp.maximum(first[0], second[0])
    left = jnp.exp(first[0] - top)
    right = jnp.exp(second[0] - top)
    return (
        top,
        first[1] * left + second[1] * right,
        first[2] * left[..., None] + second[2] * right[..., None],
    )


def per_device(prompts, kv_weight, lengths, piece_owner, piece_slot, queries, decode_key_value):
    shards = lax.axis_size(("seq", "section"))
    sender = lax.axis_index(("seq", "section"))
    tok_rows = prompts.shape[0]
    local_kv = kv_weight.shape[2]
    per_sender = shards // 2
    piece_len = tok_rows // per_sender
    cache_block = lax.all_gather(kv_weight, ("seq", "section"), axis=0, tiled=True)
    flat = cache_block.reshape(cache_block.shape[0], 2 * local_kv)
    summed = jnp.dot(prompts, flat, preferred_element_type=jnp.float32)
    fresh_entries = summed.astype(jnp.bfloat16).reshape(tok_rows, 2, local_kv)
    pieces = fresh_entries.reshape(per_sender, piece_len * 2 * local_kv)
    my_owners = lax.dynamic_slice_in_dim(piece_owner, sender * per_sender, per_sender)
    owner_range = jnp.arange(shards, dtype=jnp.int32)
    targets = (owner_range[:, None] == my_owners[None, :]).astype(jnp.bfloat16)
    outgoing = jnp.dot(targets, pieces, preferred_element_type=jnp.float32).astype(jnp.bfloat16)
    arrived = lax.all_to_all(outgoing, ("seq", "section"), split_axis=0, concat_axis=0, tiled=True)
    piece_ids = jnp.arange(piece_owner.shape[0], dtype=jnp.int32)
    matched = (
        (piece_owner == sender)[None, :] & (piece_slot[None, :] == owner_range[:, None])
    ).astype(jnp.int32)
    from_sender = jnp.sum(matched.reshape(shards, shards, per_sender), axis=2).astype(jnp.bfloat16)
    cache_local = jnp.dot(from_sender, arrived, preferred_element_type=jnp.float32).astype(
        jnp.bfloat16
    )
    cache_local = cache_local.reshape(shards * piece_len, 2, local_kv)
    has_piece = jnp.sum(matched, axis=1)
    first_token = jnp.sum(matched * piece_ids[None, :], axis=1) * piece_len
    slot_token = (first_token[:, None] + jnp.arange(piece_len, dtype=jnp.int32)[None, :]).reshape(
        -1
    )
    ends = jnp.cumsum(lengths)
    token_request = jnp.sum((slot_token[:, None] >= ends[None, :]).astype(jnp.int32), axis=1)
    filled = jnp.repeat(has_piece > 0, piece_len)
    slot_request = jnp.where(filled, token_request, -1)
    rows = queries.shape[0]
    kv_heads = local_kv // HEAD_SIZE
    query_group = queries.shape[1] // (kv_heads * HEAD_SIZE)
    scale = HEAD_SIZE ** (-0.5)
    asked_rows = queries.reshape(rows, kv_heads, query_group, HEAD_SIZE)
    cache_keys = cache_local[:, 0].reshape(-1, kv_heads, HEAD_SIZE)
    cache_values = cache_local[:, 1].reshape(-1, kv_heads, HEAD_SIZE)
    scores = (
        jnp.einsum("rgjd,cgd->rgjc", asked_rows, cache_keys, preferred_element_type=jnp.float32)
        * scale
    )
    row_request = jnp.arange(rows, dtype=jnp.int32) // DECODE_STEPS
    allowed = (slot_request[None, :] == row_request[:, None])[:, None, None, :]
    highest, total, weights = partial_softmax(scores, allowed)
    weighted = jnp.einsum(
        "rgjc,cgd->rgjd", weights, cache_values, preferred_element_type=jnp.float32
    )
    requests = rows // DECODE_STEPS
    asked_fresh_rows = queries.reshape(requests, DECODE_STEPS, kv_heads, query_group, HEAD_SIZE)
    fresh_key_rows = decode_key_value[:, 0].reshape(requests, DECODE_STEPS, kv_heads, HEAD_SIZE)
    fresh_value_rows = decode_key_value[:, 1].reshape(requests, DECODE_STEPS, kv_heads, HEAD_SIZE)
    new_scores = (
        jnp.einsum(
            "rtgjd,rsgd->rtgjs",
            asked_fresh_rows,
            fresh_key_rows,
            preferred_element_type=jnp.float32,
        )
        * scale
    )
    steps_range = jnp.arange(DECODE_STEPS, dtype=jnp.int32)
    causal = (steps_range[:, None] >= steps_range[None, :])[None, :, None, None, :]
    fresh_maximum, fresh_total_sum, new_weights = partial_softmax(new_scores, causal)
    fresh_weight_sum = jnp.einsum(
        "rtgjs,rsgd->rtgjd", new_weights, fresh_value_rows, preferred_element_type=jnp.float32
    )
    new_part = (
        fresh_maximum.reshape(rows, kv_heads, query_group),
        fresh_total_sum.reshape(rows, kv_heads, query_group),
        fresh_weight_sum.reshape(rows, kv_heads, query_group, HEAD_SIZE),
    )
    top = lax.pmax(highest, ("seq", "section"))
    group_factor = jnp.exp(highest - top)
    total_sum, weighted_sum = lax.psum(
        (total * group_factor, weighted * group_factor[..., None]), ("seq", "section")
    )
    owners_part = (top, total_sum, weighted_sum)
    final = join_parts(owners_part, new_part)
    attended = (
        (final[2] / final[1][..., None])
        .astype(jnp.bfloat16)
        .reshape(rows, kv_heads * query_group * HEAD_SIZE)
    )
    return (cache_local, attended)


MESH = pl.DeviceIdType.MESH


def project_kernel(
    chips,
    planes,
    prompts,
    weight,
    fresh,
    gathered,
    mine,
    theirs,
    from_sibling,
    summed,
    reduced,
    own_sem,
    send_sem,
    plane_send_sem,
    sum_send_sem,
    fresh_send_sem,
    line_sem,
    plane_sem,
    sibling_sem,
    reduce_sem,
    fresh_sem,
    fresh_sibling_sem,
):
    z = lax.axis_index("seq")
    t = lax.axis_index("tensor")
    c = lax.axis_index("section")
    other = 1 - c
    me = z * 2 + c
    piece = prompts.shape[1]
    depth = weight.shape[0]
    half = weight.shape[1] // 2
    rows = 2 * planes * piece

    def at(seq, tensor, section):
        return {"seq": seq, "tensor": tensor, "section": section}

    def remote(src, dst, ssem, rsem, where):
        return pltpu.make_async_remote_copy(
            src_ref=src,
            dst_ref=dst,
            send_sem=ssem,
            recv_sem=rsem,
            device_id=where,
            device_id_type=MESH,
        )

    barrier = pltpu.get_barrier_semaphore()
    for d in range(1, chips):
        for s in range(2):
            pl.semaphore_signal(
                barrier, inc=1, device_id=at(lax.rem(z + d, chips), t, s), device_id_type=MESH
            )
    for d in range(1, planes):
        pl.semaphore_signal(
            barrier, inc=1, device_id=at(z, lax.rem(t + d, planes), c), device_id_type=MESH
        )
    pl.semaphore_signal(barrier, inc=1, device_id=at(z, t, other), device_id_type=MESH)

    def columns(k):
        return pl.ds(pl.multiple_of(k * depth, depth), depth)

    own = pltpu.make_async_copy(
        prompts.at[:, :, columns(me)], gathered.at[pl.ds(me * planes, planes)], own_sem
    )
    own.start()
    pl.semaphore_wait(barrier, 2 * (chips - 1) + planes)

    sends = []
    copy = remote(
        prompts.at[:, :, columns(z * 2 + other)],
        gathered.at[pl.ds(me * planes, planes)],
        send_sem.at[0],
        line_sem.at[me],
        at(z, t, other),
    )
    copy.start()
    sends.append(copy)
    for d in range(1, chips):
        zt = lax.rem(z + d, chips)
        for s in range(2):
            copy = remote(
                prompts.at[t, :, columns(zt * 2 + s)],
                gathered.at[me * planes + t],
                send_sem.at[2 * d - 1 + s],
                line_sem.at[me],
                at(zt, t, s),
            )
            copy.start()
            sends.append(copy)

    def forward(d):
        zs = lax.rem(z + chips - d, chips)
        for s in range(2):
            src = zs * 2 + s
            slot = src * planes + t
            remote(
                gathered.at[slot],
                gathered.at[slot],
                send_sem.at[0],
                line_sem.at[src],
                at(z, t, other),
            ).wait_recv()
            for e in range(1, planes):
                copy = remote(
                    gathered.at[slot],
                    gathered.at[slot],
                    plane_send_sem.at[d - 1, s, e - 1],
                    plane_sem.at[src, t],
                    at(z, lax.rem(t + e, planes), c),
                )
                copy.start()
                sends.append(copy)

    def multiply(d):
        zs = lax.rem(z + chips - d, chips)
        if d == 0:
            own.wait()
            sibling = pl.ds((z * 2 + other) * planes, planes)
            remote(
                gathered.at[sibling],
                gathered.at[sibling],
                send_sem.at[0],
                line_sem.at[z * 2 + other],
                at(z, t, other),
            ).wait_recv()
        else:
            for s in range(2):
                src = zs * 2 + s
                for e in range(1, planes):
                    te = lax.rem(t + e, planes)
                    slot = src * planes + te
                    remote(
                        gathered.at[slot],
                        gathered.at[slot],
                        send_sem.at[0],
                        plane_sem.at[src, te],
                        at(z, te, c),
                    ).wait_recv()
        left = gathered[pl.ds(zs * 2 * planes, 2 * planes)].reshape(rows, depth)
        theirs[d] = jnp.dot(
            left,
            weight[:, pl.ds(pl.multiple_of(other * half, half), half)],
            preferred_element_type=jnp.float32,
        )
        copy = remote(
            theirs.at[d],
            from_sibling.at[d],
            sum_send_sem.at[0, d],
            sibling_sem.at[d],
            at(z, t, other),
        )
        copy.start()
        sends.append(copy)
        mine[d] = jnp.dot(
            left,
            weight[:, pl.ds(pl.multiple_of(c * half, half), half)],
            preferred_element_type=jnp.float32,
        )
        return copy

    def pass_on(d, copy):
        zs = lax.rem(z + chips - d, chips)
        copy.wait_recv()
        if d == 0:
            return
        summed[d - 1] = mine[d] + from_sibling[d]
        out = remote(
            summed.at[d - 1],
            reduced.at[d - 1],
            sum_send_sem.at[1, d],
            reduce_sem.at[d - 1],
            at(zs, t, c),
        )
        out.start()
        sends.append(out)
        return out

    outs = []
    held = multiply(0)
    for d in range(1, chips):
        forward(d)
        if d == 1:
            pass_on(0, held)
        else:
            later = multiply(d - 1)
            outs.append(pass_on(d - 1, later))
    held = multiply(chips - 1)
    outs.append(pass_on(chips - 1, held))

    total = mine[0] + from_sibling[0]
    for d in range(1, chips):
        outs[d - 1].wait_recv()
        total = total + reduced[d - 1]
    block = pl.ds(pl.multiple_of(z * rows, rows), rows)
    fresh[c, block] = total.astype(jnp.bfloat16)
    for d in range(1, chips):
        copy = remote(
            fresh.at[c, block],
            fresh.at[c, block],
            fresh_send_sem.at[0, d],
            fresh_sem.at[z],
            at(lax.rem(z + d, chips), t, c),
        )
        copy.start()
        sends.append(copy)
    for d in range(chips):
        zs = lax.rem(z + chips - d, chips)
        arrived = pl.ds(pl.multiple_of(zs * rows, rows), rows)
        if d > 0:
            remote(
                fresh.at[c, arrived],
                fresh.at[c, arrived],
                send_sem.at[0],
                fresh_sem.at[zs],
                at(z, t, other),
            ).wait_recv()
        copy = remote(
            fresh.at[c, arrived],
            fresh.at[c, arrived],
            fresh_send_sem.at[1, d],
            fresh_sibling_sem.at[zs],
            at(z, t, other),
        )
        copy.start()
        sends.append(copy)
    for d in range(chips):
        zs = lax.rem(z + chips - d, chips)
        arrived = pl.ds(pl.multiple_of(zs * rows, rows), rows)
        remote(
            fresh.at[other, arrived],
            fresh.at[other, arrived],
            send_sem.at[0],
            fresh_sibling_sem.at[zs],
            at(z, t, other),
        ).wait_recv()
    for copy in sends:
        copy.wait_send()


def project(prompts, weight, chips, planes):
    tok_rows, width = prompts.shape
    depth = weight.shape[0]
    half = weight.shape[1] // 2
    piece = tok_rows // planes
    rows = 2 * tok_rows
    shards = 2 * chips
    f32 = jnp.float32
    dma = pltpu.SemaphoreType.DMA
    return pl.pallas_call(
        functools.partial(project_kernel, chips, planes),
        out_shape=jax.ShapeDtypeStruct((2, chips * rows, half), jnp.bfloat16),
        in_specs=[
            pl.BlockSpec(memory_space=pl.ANY),
            pl.BlockSpec(memory_space=pltpu.VMEM),
        ],
        out_specs=pl.BlockSpec(memory_space=pltpu.VMEM),
        scratch_shapes=[
            pltpu.VMEM((shards * planes, piece, depth), jnp.bfloat16),
            pltpu.VMEM((chips, rows, half), f32),
            pltpu.VMEM((chips, rows, half), f32),
            pltpu.VMEM((chips, rows, half), f32),
            pltpu.VMEM((chips - 1, rows, half), f32),
            pltpu.VMEM((chips - 1, rows, half), f32),
            dma,
            dma((2 * chips - 1,)),
            dma((chips - 1, 2, planes - 1)),
            dma((2, chips)),
            dma((2, chips)),
            dma((shards,)),
            dma((shards, planes)),
            dma((chips,)),
            dma((chips - 1,)),
            dma((chips,)),
            dma((chips,)),
        ],
        compiler_params=pltpu.CompilerParams(
            collective_id=0, has_side_effects=True, vmem_limit_bytes=40 * 2**20
        ),
        name="project",
    )(prompts.reshape(planes, piece, width), weight)


TILE_REQUESTS = 8
TOKEN_BLOCK = 256


def attend_kernel(
    piece,
    owners,
    lengths,
    piece_owner,
    piece_slot,
    fresh,
    queries,
    decode,
    cache,
    attended,
    ends,
    source,
    score,
    piece_top,
    piece_factor,
    owner_of,
    values_across,
    weighted,
):
    requests = lengths.shape[0]
    pieces = piece_owner.shape[0]
    tile_rows = TILE_REQUESTS * DECODE_STEPS
    kv_heads = fresh.shape[2] // HEAD_SIZE
    local = fresh.shape[2]
    group = queries.shape[1] // (kv_heads * HEAD_SIZE)
    lanes = group * tile_rows
    per_block = TOKEN_BLOCK // piece
    scale = HEAD_SIZE ** (-0.5)
    me = lax.axis_index("seq") * lax.axis_size("section") + lax.axis_index("section")

    ends[0] = 0

    def add_length(r, total):
        total = total + lengths[r]
        ends[r + 1] = total
        return total

    lax.fori_loop(0, requests, add_length, jnp.int32(0))

    slots = source.shape[0]
    for j in range(slots):
        source[j] = -1

    def place(p, carry):
        @pl.when(piece_owner[p] == me)
        def _():
            source[piece_slot[p]] = p

        return carry

    lax.fori_loop(0, pieces, place, 0)
    for j in range(slots):
        p = source[j]
        into = pl.ds(j * piece, piece)

        @pl.when(p >= 0)
        def _():
            rows = pl.ds(pl.multiple_of(p * piece, piece), piece)
            cache[into, 0] = fresh[0, rows]
            cache[into, 1] = fresh[1, rows]

        @pl.when(p < 0)
        def _():
            cache[into] = jnp.zeros((piece, 2, local), cache.dtype)

    f32, bf16 = jnp.float32, jnp.bfloat16
    blocks = owner_of.shape[0]
    for b in range(blocks):
        for q in range(per_block):
            owner_of[b, q : q + 1] = jnp.full((1, lanes), piece_owner[b * per_block + q], jnp.int32)
        span = slice(b * TOKEN_BLOCK, (b + 1) * TOKEN_BLOCK)
        for g in range(kv_heads):
            turned = fresh[1, span, g * HEAD_SIZE : (g + 1) * HEAD_SIZE].T
            values_across[g, b, :, :TOKEN_BLOCK] = turned
            values_across[g, b, :, TOKEN_BLOCK:] = turned
    lane_row = lax.broadcasted_iota(jnp.int32, (1, lanes), 1) % tile_rows
    lane_request = lane_row // DECODE_STEPS
    token = lax.broadcasted_iota(jnp.int32, (TOKEN_BLOCK, lanes), 0)
    new_row = lax.broadcasted_iota(jnp.int32, (tile_rows, lanes), 0)
    new_mask = (new_row // DECODE_STEPS == lane_request) & (new_row <= lane_row)

    def outer(a, b):
        return lax.dot_general(a, b, (((1,), (1,)), ((), ())), preferred_element_type=f32)

    def inner(a, b):
        return lax.dot_general(a, b, (((0,), (0,)), ((), ())), preferred_element_type=f32)

    def tile(i, carry):
        first = i * TILE_REQUESTS
        begin = jnp.zeros((1, lanes), jnp.int32)
        end = jnp.zeros((1, lanes), jnp.int32)
        for r in range(TILE_REQUESTS):
            begin = jnp.where(lane_request == r, ends[first + r], begin)
            end = jnp.where(lane_request == r, ends[first + r + 1], end)
        low = ends[first] // TOKEN_BLOCK
        high = (ends[first + TILE_REQUESTS] + TOKEN_BLOCK - 1) // TOKEN_BLOCK
        rows = pl.ds(pl.multiple_of(i * tile_rows, tile_rows), tile_rows)
        asked = []
        for g in range(kv_heads):
            asked.append(
                jnp.concatenate(
                    [
                        queries[rows, (g * group + j) * HEAD_SIZE : (g * group + j + 1) * HEAD_SIZE]
                        for j in range(group)
                    ],
                    axis=0,
                )
            )
        piece_top[...] = jnp.full(piece_top.shape, masked_value, f32)

        def scores(b, carry):
            where = token + b * TOKEN_BLOCK
            allowed = (where >= begin) & (where < end)
            span = pl.ds(pl.multiple_of(b * TOKEN_BLOCK, TOKEN_BLOCK), TOKEN_BLOCK)
            for g in range(kv_heads):
                head = slice(g * HEAD_SIZE, (g + 1) * HEAD_SIZE)
                s = jnp.where(allowed, outer(fresh[0, span, head], asked[g]) * scale, masked_value)
                score[g, span] = s
                piece_top[g, b] = jnp.max(s.reshape(per_block, piece, lanes), axis=1)
            return carry

        lax.fori_loop(low, high, scores, 0)

        starts = []
        for g in range(kv_heads):
            keys = decode[rows, 0, g * HEAD_SIZE : (g + 1) * HEAD_SIZE]
            values = decode[rows, 1, g * HEAD_SIZE : (g + 1) * HEAD_SIZE]
            s = jnp.where(new_mask, outer(keys, asked[g]) * scale, masked_value)
            new_top = jnp.max(s, axis=0, keepdims=True)
            p = jnp.where(new_mask, jnp.exp(s - new_top), 0.0)
            highest = piece_top[g]
            top = jnp.maximum(new_top, jnp.max(highest, axis=(0, 1))[None, :])
            for o in range(owners):
                mine = owner_of[...] == o
                most = jnp.max(jnp.where(mine, highest, masked_value), axis=(0, 1))
                highest = jnp.where(mine, most[None, None, :], highest)
            piece_top[g] = highest
            piece_factor[g] = jnp.exp(highest - top[None])
            factor = jnp.exp(new_top - top)
            weighted[g] = inner(values, p.astype(bf16)) * factor
            starts.append(jnp.sum(p, axis=0, keepdims=True) * factor)

        def weigh(b, totals):
            span = pl.ds(pl.multiple_of(b * TOKEN_BLOCK, TOKEN_BLOCK), TOKEN_BLOCK)
            results = []
            for g in range(kv_heads):
                s = score[g, span].reshape(per_block, piece, lanes)
                factor = piece_factor[g, b]
                p = jnp.exp(s - piece_top[g, b][:, None, :])
                w = p.astype(bf16).astype(f32) * factor[:, None, :]
                w = w.reshape(TOKEN_BLOCK, lanes)
                upper = w.astype(bf16)
                lower = (w - upper.astype(f32)).astype(bf16)
                weighted[g] += jnp.dot(
                    values_across[g, b],
                    jnp.concatenate([upper, lower], axis=0),
                    preferred_element_type=f32,
                )
                sums = jnp.sum(p, axis=1) * factor
                results.append(totals[g] + jnp.sum(sums, axis=0, keepdims=True))
            return tuple(results)

        totals = lax.fori_loop(low, high, weigh, tuple(starts))
        for g in range(kv_heads):
            result = (weighted[g] / totals[g]).T.astype(bf16)
            for j in range(group):
                attended[rows, (g * group + j) * HEAD_SIZE : (g * group + j + 1) * HEAD_SIZE] = result[
                    j * tile_rows : (j + 1) * tile_rows
                ]
        return carry

    lax.fori_loop(0, requests // TILE_REQUESTS, tile, 0)


def attend(lengths, piece_owner, piece_slot, fresh, queries, decode, shards):
    tokens = fresh.shape[1]
    local = fresh.shape[2]
    piece = tokens // piece_owner.shape[0]
    slots = shards
    blocks = tokens // TOKEN_BLOCK
    kv_heads = local // HEAD_SIZE
    group = queries.shape[1] // local
    lanes = group * TILE_REQUESTS * DECODE_STEPS
    smem = pl.BlockSpec(memory_space=pltpu.SMEM)
    vmem = pl.BlockSpec(memory_space=pltpu.VMEM)
    return pl.pallas_call(
        functools.partial(attend_kernel, piece, shards),
        out_shape=(
            jax.ShapeDtypeStruct((slots * piece, 2, local), jnp.bfloat16),
            jax.ShapeDtypeStruct(queries.shape, jnp.bfloat16),
        ),
        in_specs=[smem, smem, smem, vmem, vmem, vmem],
        out_specs=(vmem, vmem),
        scratch_shapes=[
            pltpu.SMEM((lengths.shape[0] + 1,), jnp.int32),
            pltpu.SMEM((slots,), jnp.int32),
            pltpu.VMEM((kv_heads, tokens, lanes), jnp.float32),
            pltpu.VMEM((kv_heads, blocks, TOKEN_BLOCK // piece, lanes), jnp.float32),
            pltpu.VMEM((kv_heads, blocks, TOKEN_BLOCK // piece, lanes), jnp.float32),
            pltpu.VMEM((blocks, TOKEN_BLOCK // piece, lanes), jnp.int32),
            pltpu.VMEM((kv_heads, blocks, HEAD_SIZE, 2 * TOKEN_BLOCK), jnp.bfloat16),
            pltpu.VMEM((kv_heads, HEAD_SIZE, lanes), jnp.float32),
        ],
        compiler_params=pltpu.CompilerParams(vmem_limit_bytes=32 * 2**20),
        name="attend",
    )(lengths, piece_owner, piece_slot, fresh, queries, decode)


def per_device_fused(
    mesh, prompts, kv_weight, lengths, piece_owner, piece_slot, queries, decode_key_value
):
    chips, planes = mesh.shape["seq"], mesh.shape["tensor"]
    depth, _, local = kv_weight.shape
    fresh = project(prompts, kv_weight.reshape(depth, 2 * local), chips, planes)
    cache, attended = attend(
        lengths,
        piece_owner,
        piece_slot,
        fresh,
        queries,
        decode_key_value,
        2 * chips,
    )
    return cache, attended


def fits(mesh):
    return mesh.shape["groups"] == 1 and mesh.shape["section"] == 2 and mesh.shape["seq"] <= 4


def solution(mesh):
    placed = (
        P(("groups", "seq", "section"), None),
        P(("seq", "section"), None, "tensor"),
        P("groups"),
        P("groups"),
        P("groups"),
        P("groups", "tensor"),
        P("groups", None, "tensor"),
    )
    return jax.shard_map(
        functools.partial(per_device_fused, mesh) if fits(mesh) else per_device,
        mesh=mesh,
        in_specs=placed,
        out_specs=(P(("groups", "seq", "section"), None, "tensor"), P("groups", "tensor")),
        check_vma=False,
    )
```

```python
import functools

import jax
import jax.numpy as jnp
from jax import lax
from jax.experimental import pallas as pl
from jax.experimental.pallas import tpu as pltpu
from jax.sharding import PartitionSpec as P

HEAD_SIZE = 128
DECODE_STEPS = 4


masked_value = -1e30


def partial_softmax(scores, allowed):
    highest = jnp.max(jnp.where(allowed, scores, masked_value), axis=-1)
    weights = jnp.where(allowed, jnp.exp(scores - highest[..., None]), 0.0)
    return (highest, jnp.sum(weights, axis=-1), weights.astype(jnp.bfloat16))


def join_parts(first, second):
    top = jnp.maximum(first[0], second[0])
    left = jnp.exp(first[0] - top)
    right = jnp.exp(second[0] - top)
    return (
        top,
        first[1] * left + second[1] * right,
        first[2] * left[..., None] + second[2] * right[..., None],
    )


def per_device(prompts, kv_weight, lengths, piece_owner, piece_slot, queries, decode_key_value):
    shards = lax.axis_size(("seq", "section"))
    sender = lax.axis_index(("seq", "section"))
    tok_rows = prompts.shape[0]
    local_kv = kv_weight.shape[2]
    per_sender = shards // 2
    piece_len = tok_rows // per_sender
    cache_block = lax.all_gather(kv_weight, ("seq", "section"), axis=0, tiled=True)
    flat = cache_block.reshape(cache_block.shape[0], 2 * local_kv)
    summed = jnp.dot(prompts, flat, preferred_element_type=jnp.float32)
    fresh_entries = summed.astype(jnp.bfloat16).reshape(tok_rows, 2, local_kv)
    pieces = fresh_entries.reshape(per_sender, piece_len * 2 * local_kv)
    my_owners = lax.dynamic_slice_in_dim(piece_owner, sender * per_sender, per_sender)
    owner_range = jnp.arange(shards, dtype=jnp.int32)
    targets = (owner_range[:, None] == my_owners[None, :]).astype(jnp.bfloat16)
    outgoing = jnp.dot(targets, pieces, preferred_element_type=jnp.float32).astype(jnp.bfloat16)
    arrived = lax.all_to_all(outgoing, ("seq", "section"), split_axis=0, concat_axis=0, tiled=True)
    piece_ids = jnp.arange(piece_owner.shape[0], dtype=jnp.int32)
    matched = (
        (piece_owner == sender)[None, :] & (piece_slot[None, :] == owner_range[:, None])
    ).astype(jnp.int32)
    from_sender = jnp.sum(matched.reshape(shards, shards, per_sender), axis=2).astype(jnp.bfloat16)
    cache_local = jnp.dot(from_sender, arrived, preferred_element_type=jnp.float32).astype(
        jnp.bfloat16
    )
    cache_local = cache_local.reshape(shards * piece_len, 2, local_kv)
    has_piece = jnp.sum(matched, axis=1)
    first_token = jnp.sum(matched * piece_ids[None, :], axis=1) * piece_len
    slot_token = (first_token[:, None] + jnp.arange(piece_len, dtype=jnp.int32)[None, :]).reshape(
        -1
    )
    ends = jnp.cumsum(lengths)
    token_request = jnp.sum((slot_token[:, None] >= ends[None, :]).astype(jnp.int32), axis=1)
    filled = jnp.repeat(has_piece > 0, piece_len)
    slot_request = jnp.where(filled, token_request, -1)
    rows = queries.shape[0]
    kv_heads = local_kv // HEAD_SIZE
    query_group = queries.shape[1] // (kv_heads * HEAD_SIZE)
    scale = HEAD_SIZE ** (-0.5)
    asked_rows = queries.reshape(rows, kv_heads, query_group, HEAD_SIZE)
    cache_keys = cache_local[:, 0].reshape(-1, kv_heads, HEAD_SIZE)
    cache_values = cache_local[:, 1].reshape(-1, kv_heads, HEAD_SIZE)
    scores = (
        jnp.einsum("rgjd,cgd->rgjc", asked_rows, cache_keys, preferred_element_type=jnp.float32)
        * scale
    )
    row_request = jnp.arange(rows, dtype=jnp.int32) // DECODE_STEPS
    allowed = (slot_request[None, :] == row_request[:, None])[:, None, None, :]
    highest, total, weights = partial_softmax(scores, allowed)
    weighted = jnp.einsum(
        "rgjc,cgd->rgjd", weights, cache_values, preferred_element_type=jnp.float32
    )
    requests = rows // DECODE_STEPS
    asked_fresh_rows = queries.reshape(requests, DECODE_STEPS, kv_heads, query_group, HEAD_SIZE)
    fresh_key_rows = decode_key_value[:, 0].reshape(requests, DECODE_STEPS, kv_heads, HEAD_SIZE)
    fresh_value_rows = decode_key_value[:, 1].reshape(requests, DECODE_STEPS, kv_heads, HEAD_SIZE)
    new_scores = (
        jnp.einsum(
            "rtgjd,rsgd->rtgjs",
            asked_fresh_rows,
            fresh_key_rows,
            preferred_element_type=jnp.float32,
        )
        * scale
    )
    steps_range = jnp.arange(DECODE_STEPS, dtype=jnp.int32)
    causal = (steps_range[:, None] >= steps_range[None, :])[None, :, None, None, :]
    fresh_maximum, fresh_total_sum, new_weights = partial_softmax(new_scores, causal)
    fresh_weight_sum = jnp.einsum(
        "rtgjs,rsgd->rtgjd", new_weights, fresh_value_rows, preferred_element_type=jnp.float32
    )
    new_part = (
        fresh_maximum.reshape(rows, kv_heads, query_group),
        fresh_total_sum.reshape(rows, kv_heads, query_group),
        fresh_weight_sum.reshape(rows, kv_heads, query_group, HEAD_SIZE),
    )
    top = lax.pmax(highest, ("seq", "section"))
    group_factor = jnp.exp(highest - top)
    total_sum, weighted_sum = lax.psum(
        (total * group_factor, weighted * group_factor[..., None]), ("seq", "section")
    )
    owners_part = (top, total_sum, weighted_sum)
    final = join_parts(owners_part, new_part)
    attended = (
        (final[2] / final[1][..., None])
        .astype(jnp.bfloat16)
        .reshape(rows, kv_heads * query_group * HEAD_SIZE)
    )
    return (cache_local, attended)


MESH = pl.DeviceIdType.MESH


def project_kernel(
    chips,
    planes,
    prompts,
    weight,
    fresh,
    gathered,
    mine,
    theirs,
    from_sibling,
    summed,
    reduced,
    own_sem,
    send_sem,
    plane_send_sem,
    sum_send_sem,
    fresh_send_sem,
    line_sem,
    plane_sem,
    sibling_sem,
    reduce_sem,
    fresh_sem,
    fresh_sibling_sem,
):
    z = lax.axis_index("seq")
    t = lax.axis_index("tensor")
    c = lax.axis_index("section")
    other = 1 - c
    me = z * 2 + c
    piece = prompts.shape[1]
    depth = weight.shape[0]
    half = weight.shape[1] // 2
    rows = 2 * planes * piece

    def at(seq, tensor, section):
        return {"seq": seq, "tensor": tensor, "section": section}

    def remote(src, dst, ssem, rsem, where):
        return pltpu.make_async_remote_copy(
            src_ref=src,
            dst_ref=dst,
            send_sem=ssem,
            recv_sem=rsem,
            device_id=where,
            device_id_type=MESH,
        )

    barrier = pltpu.get_barrier_semaphore()
    for d in range(1, chips):
        for s in range(2):
            pl.semaphore_signal(
                barrier, inc=1, device_id=at(lax.rem(z + d, chips), t, s), device_id_type=MESH
            )
    for d in range(1, planes):
        pl.semaphore_signal(
            barrier, inc=1, device_id=at(z, lax.rem(t + d, planes), c), device_id_type=MESH
        )
    pl.semaphore_signal(barrier, inc=1, device_id=at(z, t, other), device_id_type=MESH)

    def columns(k):
        return pl.ds(pl.multiple_of(k * depth, depth), depth)

    own = pltpu.make_async_copy(
        prompts.at[:, :, columns(me)], gathered.at[pl.ds(me * planes, planes)], own_sem
    )
    own.start()
    pl.semaphore_wait(barrier, 2 * (chips - 1) + planes)

    sends = []
    copy = remote(
        prompts.at[:, :, columns(z * 2 + other)],
        gathered.at[pl.ds(me * planes, planes)],
        send_sem.at[0],
        line_sem.at[me],
        at(z, t, other),
    )
    copy.start()
    sends.append(copy)
    for d in range(1, chips):
        zt = lax.rem(z + d, chips)
        for s in range(2):
            copy = remote(
                prompts.at[t, :, columns(zt * 2 + s)],
                gathered.at[me * planes + t],
                send_sem.at[2 * d - 1 + s],
                line_sem.at[me],
                at(zt, t, s),
            )
            copy.start()
            sends.append(copy)

    def forward(d):
        zs = lax.rem(z + chips - d, chips)
        for s in range(2):
            src = zs * 2 + s
            slot = src * planes + t
            remote(
                gathered.at[slot],
                gathered.at[slot],
                send_sem.at[0],
                line_sem.at[src],
                at(z, t, other),
            ).wait_recv()
            for e in range(1, planes):
                copy = remote(
                    gathered.at[slot],
                    gathered.at[slot],
                    plane_send_sem.at[d - 1, s, e - 1],
                    plane_sem.at[src, t],
                    at(z, lax.rem(t + e, planes), c),
                )
                copy.start()
                sends.append(copy)

    def multiply(d):
        zs = lax.rem(z + chips - d, chips)
        if d == 0:
            own.wait()
            sibling = pl.ds((z * 2 + other) * planes, planes)
            remote(
                gathered.at[sibling],
                gathered.at[sibling],
                send_sem.at[0],
                line_sem.at[z * 2 + other],
                at(z, t, other),
            ).wait_recv()
        else:
            for s in range(2):
                src = zs * 2 + s
                for e in range(1, planes):
                    te = lax.rem(t + e, planes)
                    slot = src * planes + te
                    remote(
                        gathered.at[slot],
                        gathered.at[slot],
                        send_sem.at[0],
                        plane_sem.at[src, te],
                        at(z, te, c),
                    ).wait_recv()
        left = gathered[pl.ds(zs * 2 * planes, 2 * planes)].reshape(rows, depth)
        theirs[d] = jnp.dot(
            left,
            weight[:, pl.ds(pl.multiple_of(other * half, half), half)],
            preferred_element_type=jnp.float32,
        )
        copy = remote(
            theirs.at[d],
            from_sibling.at[d],
            sum_send_sem.at[0, d],
            sibling_sem.at[d],
            at(z, t, other),
        )
        copy.start()
        sends.append(copy)
        mine[d] = jnp.dot(
            left,
            weight[:, pl.ds(pl.multiple_of(c * half, half), half)],
            preferred_element_type=jnp.float32,
        )
        return copy

    def pass_on(d, copy):
        zs = lax.rem(z + chips - d, chips)
        copy.wait_recv()
        if d == 0:
            return
        summed[d - 1] = mine[d] + from_sibling[d]
        pair = []
        for h in range(2):
            part = pl.ds(h * (rows // 2), rows // 2)
            out = remote(
                summed.at[d - 1, part],
                reduced.at[d - 1, part],
                sum_send_sem.at[1 + h, d],
                reduce_sem.at[h, d - 1],
                at(zs, t, c),
            )
            out.start()
            sends.append(out)
            pair.append(out)
        return pair

    outs = []
    held = multiply(0)
    for d in range(1, chips):
        forward(d)
        if d == 1:
            pass_on(0, held)
        else:
            later = multiply(d - 1)
            outs.append(pass_on(d - 1, later))
    held = multiply(chips - 1)
    outs.append(pass_on(chips - 1, held))

    size = rows // 2

    def part_of(zs, h):
        return pl.ds(pl.multiple_of(zs * rows + h * size, size), size)

    for h in range(2):
        part = slice(h * size, (h + 1) * size)
        total = mine[0, part] + from_sibling[0, part]
        for d in range(1, chips):
            outs[d - 1][h].wait_recv()
            total = total + reduced[d - 1, part]
        fresh[c, part_of(z, h)] = total.astype(jnp.bfloat16)
        block = fresh.at[c, part_of(z, h)]
        for d in range(1, chips):
            copy = remote(
                block,
                block,
                fresh_send_sem.at[0, h, d],
                fresh_sem.at[h, z],
                at(lax.rem(z + d, chips), t, c),
            )
            copy.start()
            sends.append(copy)
    for h in range(2):
        for d in range(chips):
            zs = lax.rem(z + chips - d, chips)
            block = fresh.at[c, part_of(zs, h)]
            copy = remote(
                block,
                block,
                fresh_send_sem.at[1, h, d],
                fresh_sibling_sem.at[h, zs],
                at(z, t, other),
            )
            if d > 0:
                remote(
                    block, block, send_sem.at[0], fresh_sem.at[h, zs], at(z, t, other)
                ).wait_recv()
            copy.start()
            sends.append(copy)
    for h in range(2):
        for d in range(chips):
            zs = lax.rem(z + chips - d, chips)
            block = fresh.at[other, part_of(zs, h)]
            remote(
                block, block, send_sem.at[0], fresh_sibling_sem.at[h, zs], at(z, t, other)
            ).wait_recv()
    for copy in sends:
        copy.wait_send()


def project(prompts, weight, chips, planes):
    tok_rows, width = prompts.shape
    depth = weight.shape[0]
    half = weight.shape[1] // 2
    piece = tok_rows // planes
    rows = 2 * tok_rows
    shards = 2 * chips
    f32 = jnp.float32
    dma = pltpu.SemaphoreType.DMA
    return pl.pallas_call(
        functools.partial(project_kernel, chips, planes),
        out_shape=jax.ShapeDtypeStruct((2, chips * rows, half), jnp.bfloat16),
        in_specs=[
            pl.BlockSpec(memory_space=pl.ANY),
            pl.BlockSpec(memory_space=pltpu.VMEM),
        ],
        out_specs=pl.BlockSpec(memory_space=pltpu.VMEM),
        scratch_shapes=[
            pltpu.VMEM((shards * planes, piece, depth), jnp.bfloat16),
            pltpu.VMEM((chips, rows, half), f32),
            pltpu.VMEM((chips, rows, half), f32),
            pltpu.VMEM((chips, rows, half), f32),
            pltpu.VMEM((chips - 1, rows, half), f32),
            pltpu.VMEM((chips - 1, rows, half), f32),
            dma,
            dma((2 * chips - 1,)),
            dma((chips - 1, 2, planes - 1)),
            dma((3, chips)),
            dma((2, 2, chips)),
            dma((shards,)),
            dma((shards, planes)),
            dma((chips,)),
            dma((2, chips - 1)),
            dma((2, chips)),
            dma((2, chips)),
        ],
        compiler_params=pltpu.CompilerParams(
            collective_id=0, has_side_effects=True, vmem_limit_bytes=40 * 2**20
        ),
        name="project",
    )(prompts.reshape(planes, piece, width), weight)


TILE_REQUESTS = 8
TOKEN_BLOCK = 256


def attend_kernel(
    piece,
    owners,
    lengths,
    piece_owner,
    piece_slot,
    fresh,
    queries,
    decode,
    cache,
    attended,
    ends,
    source,
    score,
    piece_top,
    piece_factor,
    owner_of,
    values_across,
    weighted,
):
    requests = lengths.shape[0]
    pieces = piece_owner.shape[0]
    tile_rows = TILE_REQUESTS * DECODE_STEPS
    kv_heads = fresh.shape[2] // HEAD_SIZE
    local = fresh.shape[2]
    group = queries.shape[1] // (kv_heads * HEAD_SIZE)
    lanes = group * tile_rows
    per_block = TOKEN_BLOCK // piece
    scale = HEAD_SIZE ** (-0.5)
    me = lax.axis_index("seq") * lax.axis_size("section") + lax.axis_index("section")

    ends[0] = 0

    def add_length(r, total):
        total = total + lengths[r]
        ends[r + 1] = total
        return total

    lax.fori_loop(0, requests, add_length, jnp.int32(0))

    slots = source.shape[0]
    for j in range(slots):
        source[j] = -1

    def place(p, carry):
        @pl.when(piece_owner[p] == me)
        def _():
            source[piece_slot[p]] = p

        return carry

    lax.fori_loop(0, pieces, place, 0)
    for j in range(slots):
        p = source[j]
        into = pl.ds(j * piece, piece)

        @pl.when(p >= 0)
        def _():
            rows = pl.ds(pl.multiple_of(p * piece, piece), piece)
            cache[into, 0] = fresh[0, rows]
            cache[into, 1] = fresh[1, rows]

        @pl.when(p < 0)
        def _():
            cache[into] = jnp.zeros((piece, 2, local), cache.dtype)

    f32, bf16 = jnp.float32, jnp.bfloat16
    blocks = owner_of.shape[0]
    for b in range(blocks):
        for q in range(per_block):
            owner_of[b, q : q + 1] = jnp.full((1, lanes), piece_owner[b * per_block + q], jnp.int32)
        span = slice(b * TOKEN_BLOCK, (b + 1) * TOKEN_BLOCK)
        for g in range(kv_heads):
            turned = fresh[1, span, g * HEAD_SIZE : (g + 1) * HEAD_SIZE].T
            values_across[g, b, :, :TOKEN_BLOCK] = turned
            values_across[g, b, :, TOKEN_BLOCK:] = turned
    lane_row = lax.broadcasted_iota(jnp.int32, (1, lanes), 1) % tile_rows
    lane_request = lane_row // DECODE_STEPS
    token = lax.broadcasted_iota(jnp.int32, (TOKEN_BLOCK, lanes), 0)
    new_row = lax.broadcasted_iota(jnp.int32, (tile_rows, lanes), 0)
    new_mask = (new_row // DECODE_STEPS == lane_request) & (new_row <= lane_row)

    def outer(a, b):
        return lax.dot_general(a, b, (((1,), (1,)), ((), ())), preferred_element_type=f32)

    def inner(a, b):
        return lax.dot_general(a, b, (((0,), (0,)), ((), ())), preferred_element_type=f32)

    def tile(i, carry):
        first = i * TILE_REQUESTS
        begin = jnp.zeros((1, lanes), jnp.int32)
        end = jnp.zeros((1, lanes), jnp.int32)
        for r in range(TILE_REQUESTS):
            begin = jnp.where(lane_request == r, ends[first + r], begin)
            end = jnp.where(lane_request == r, ends[first + r + 1], end)
        low = ends[first] // TOKEN_BLOCK
        high = (ends[first + TILE_REQUESTS] + TOKEN_BLOCK - 1) // TOKEN_BLOCK
        rows = pl.ds(pl.multiple_of(i * tile_rows, tile_rows), tile_rows)
        asked = []
        for g in range(kv_heads):
            asked.append(
                jnp.concatenate(
                    [
                        queries[rows, (g * group + j) * HEAD_SIZE : (g * group + j + 1) * HEAD_SIZE]
                        for j in range(group)
                    ],
                    axis=0,
                )
            )
        piece_top[...] = jnp.full(piece_top.shape, masked_value, f32)

        def scores(b, carry):
            where = token + b * TOKEN_BLOCK
            allowed = (where >= begin) & (where < end)
            span = pl.ds(pl.multiple_of(b * TOKEN_BLOCK, TOKEN_BLOCK), TOKEN_BLOCK)
            for g in range(kv_heads):
                head = slice(g * HEAD_SIZE, (g + 1) * HEAD_SIZE)
                s = jnp.where(allowed, outer(fresh[0, span, head], asked[g]) * scale, masked_value)
                score[g, span] = s
                piece_top[g, b] = jnp.max(s.reshape(per_block, piece, lanes), axis=1)
            return carry

        lax.fori_loop(low, high, scores, 0)

        starts = []
        for g in range(kv_heads):
            keys = decode[rows, 0, g * HEAD_SIZE : (g + 1) * HEAD_SIZE]
            values = decode[rows, 1, g * HEAD_SIZE : (g + 1) * HEAD_SIZE]
            s = jnp.where(new_mask, outer(keys, asked[g]) * scale, masked_value)
            new_top = jnp.max(s, axis=0, keepdims=True)
            p = jnp.where(new_mask, jnp.exp(s - new_top), 0.0)
            highest = piece_top[g]
            top = jnp.maximum(new_top, jnp.max(highest, axis=(0, 1))[None, :])
            for o in range(owners):
                mine = owner_of[...] == o
                most = jnp.max(jnp.where(mine, highest, masked_value), axis=(0, 1))
                highest = jnp.where(mine, most[None, None, :], highest)
            piece_top[g] = highest
            piece_factor[g] = jnp.exp(highest - top[None])
            factor = jnp.exp(new_top - top)
            weighted[g] = inner(values, p.astype(bf16)) * factor
            starts.append(jnp.sum(p, axis=0, keepdims=True) * factor)

        def weigh(b, totals):
            span = pl.ds(pl.multiple_of(b * TOKEN_BLOCK, TOKEN_BLOCK), TOKEN_BLOCK)
            results = []
            for g in range(kv_heads):
                s = score[g, span].reshape(per_block, piece, lanes)
                factor = piece_factor[g, b]
                p = jnp.exp(s - piece_top[g, b][:, None, :])
                w = p.astype(bf16).astype(f32) * factor[:, None, :]
                w = w.reshape(TOKEN_BLOCK, lanes)
                upper = w.astype(bf16)
                lower = (w - upper.astype(f32)).astype(bf16)
                weighted[g] += jnp.dot(
                    values_across[g, b],
                    jnp.concatenate([upper, lower], axis=0),
                    preferred_element_type=f32,
                )
                sums = jnp.sum(p, axis=1) * factor
                results.append(totals[g] + jnp.sum(sums, axis=0, keepdims=True))
            return tuple(results)

        totals = lax.fori_loop(low, high, weigh, tuple(starts))
        for g in range(kv_heads):
            result = (weighted[g] / totals[g]).T.astype(bf16)
            for j in range(group):
                attended[rows, (g * group + j) * HEAD_SIZE : (g * group + j + 1) * HEAD_SIZE] = result[
                    j * tile_rows : (j + 1) * tile_rows
                ]
        return carry

    lax.fori_loop(0, requests // TILE_REQUESTS, tile, 0)


def attend(lengths, piece_owner, piece_slot, fresh, queries, decode, shards):
    tokens = fresh.shape[1]
    local = fresh.shape[2]
    piece = tokens // piece_owner.shape[0]
    slots = shards
    blocks = tokens // TOKEN_BLOCK
    kv_heads = local // HEAD_SIZE
    group = queries.shape[1] // local
    lanes = group * TILE_REQUESTS * DECODE_STEPS
    smem = pl.BlockSpec(memory_space=pltpu.SMEM)
    vmem = pl.BlockSpec(memory_space=pltpu.VMEM)
    return pl.pallas_call(
        functools.partial(attend_kernel, piece, shards),
        out_shape=(
            jax.ShapeDtypeStruct((slots * piece, 2, local), jnp.bfloat16),
            jax.ShapeDtypeStruct(queries.shape, jnp.bfloat16),
        ),
        in_specs=[smem, smem, smem, vmem, vmem, vmem],
        out_specs=(vmem, vmem),
        scratch_shapes=[
            pltpu.SMEM((lengths.shape[0] + 1,), jnp.int32),
            pltpu.SMEM((slots,), jnp.int32),
            pltpu.VMEM((kv_heads, tokens, lanes), jnp.float32),
            pltpu.VMEM((kv_heads, blocks, TOKEN_BLOCK // piece, lanes), jnp.float32),
            pltpu.VMEM((kv_heads, blocks, TOKEN_BLOCK // piece, lanes), jnp.float32),
            pltpu.VMEM((blocks, TOKEN_BLOCK // piece, lanes), jnp.int32),
            pltpu.VMEM((kv_heads, blocks, HEAD_SIZE, 2 * TOKEN_BLOCK), jnp.bfloat16),
            pltpu.VMEM((kv_heads, HEAD_SIZE, lanes), jnp.float32),
        ],
        compiler_params=pltpu.CompilerParams(vmem_limit_bytes=32 * 2**20),
        name="attend",
    )(lengths, piece_owner, piece_slot, fresh, queries, decode)


def per_device_fused(
    mesh, prompts, kv_weight, lengths, piece_owner, piece_slot, queries, decode_key_value
):
    chips, planes = mesh.shape["seq"], mesh.shape["tensor"]
    depth, _, local = kv_weight.shape
    fresh = project(prompts, kv_weight.reshape(depth, 2 * local), chips, planes)
    cache, attended = attend(
        lengths,
        piece_owner,
        piece_slot,
        fresh,
        queries,
        decode_key_value,
        2 * chips,
    )
    return cache, attended


def fits(mesh):
    return mesh.shape["groups"] == 1 and mesh.shape["section"] == 2 and mesh.shape["seq"] <= 4


def solution(mesh):
    placed = (
        P(("groups", "seq", "section"), None),
        P(("seq", "section"), None, "tensor"),
        P("groups"),
        P("groups"),
        P("groups"),
        P("groups", "tensor"),
        P("groups", None, "tensor"),
    )
    return jax.shard_map(
        functools.partial(per_device_fused, mesh) if fits(mesh) else per_device,
        mesh=mesh,
        in_specs=placed,
        out_specs=(P(("groups", "seq", "section"), None, "tensor"), P("groups", "tensor")),
        check_vma=False,
    )
```
